32 devices in a mesh: row: 4 (over y, x), col: 8 (over z, core).
Axes of the slice: x: 2, y: 2, z: 4, core: 2. Of those that a mesh axis runs over, the one named last changes fastest.
Arguments:
- landmarks: float32 [20480, 128], P(('row', 'col')), may hold values from -6 to 6
- slab_points: float32 [2048, 128], P('col'), may hold values from -6 to 6
- panel_points: float32 [2, 256, 128], replicated, may hold values from -6 to 6, as said below
- inverse_blocks: float32 [2, 256, 256], replicated, as said below
Outputs:
- updated_slab: float32 [20480, 2048], P('row', 'col')
The draws below stay inside these ranges and needn't reach their ends.
Inputs may be any that keep to these rules, and one draw needn't show every extreme that they name: `panel_points`: points of order one, at most 6 in magnitude. inverse_blocks[0] is the inverse of the lower Cholesky factor of gaussian(panel_points[0], panel_points[0]) + 0.001 I; inverse_blocks[1] is the inverse of the lower Cholesky factor of gaussian(panel_points[1], panel_points[1]) - first_next first_next^T + 0.001 I. Both are lower triangular with a positive diagonal.
All inputs are finite; a program needn't handle non-finite values.
Results may differ from the reference program's by a relative error of at most 0.0003.
Values sent between devices are 32-bit elements; how exact they have to be, the bound alone decides.
No kernel may reach another device: no remote copies, remote signals or barrier semaphores. Data moves between devices by JAX's collectives and lax.ppermute only.
A program may use at most 128 MiB of HBM per device.

```python
import jax
import jax.numpy as jnp
from jax import lax

DIM = 128
PANEL = 256
ROWS_DEV = 640
LANDMARKS = 20480
SLAB = 2048


def shared_points(key):
    point_key = jax.random.fold_in(key, 4177)
    points = jnp.clip(jax.random.normal(point_key, (2, PANEL, DIM), jnp.float32), -6.0, 6.0)
    return points


def kernel_rows(left_points, right_points):
    inner = lax.dot_general(left_points, right_points, (((1,), (1,)), ((), ())), precision=lax.Precision.HIGHEST, preferred_element_type=jnp.float32)
    left_norms = jnp.sum(left_points * left_points, axis=1)[:, None]
    right_norms = jnp.sum(right_points * right_points, axis=1)[None, :]
    return jnp.exp((2.0 * inner - left_norms - right_norms) / DIM)


def draw_panel_points(key, part):
    return shared_points(key)


def draw_inverse_blocks(key, part):
    points = shared_points(key)
    identity = jnp.eye(PANEL, dtype=jnp.float32)
    first_factor = jnp.linalg.cholesky(kernel_rows(points[0], points[0]) + 0.001 * identity)
    first_inverse = jax.scipy.linalg.solve_triangular(first_factor, identity, lower=True)
    first_next = lax.dot_general(kernel_rows(points[1], points[0]), first_inverse, (((1,), (1,)), ((), ())), precision=lax.Precision.HIGHEST, preferred_element_type=jnp.float32)
    schur_block = kernel_rows(points[1], points[1]) - lax.dot_general(first_next, first_next, (((1,), (1,)), ((), ())), precision=lax.Precision.HIGHEST, preferred_element_type=jnp.float32)
    second_factor = jnp.linalg.cholesky(schur_block + 0.001 * identity)
    second_inverse = jax.scipy.linalg.solve_triangular(second_factor, identity, lower=True)
    return jnp.stack([first_inverse, second_inverse], axis=0)


def steps_of(stream_key, shape, pieces, low, high):
    def one(dim, blocks):
        draws = jax.random.uniform(jax.random.fold_in(jax.random.fold_in(stream_key, 6), dim), (blocks,), jnp.float32, low / len(pieces), high / len(pieces))
        return jnp.repeat(jnp.exp(draws), shape[dim] // blocks).reshape((-1,) + (1,) * (len(shape) - dim - 1))

    loudness = one(*pieces[0])
    for cut in pieces[1:]:
        loudness = loudness * one(*cut)
    return loudness


def normal_values(rng, shape, spread, reach, cuts=(), held_as=jnp.bfloat16):
    drawn = jax.random.normal(rng, shape, jnp.float32) * spread
    if len(cuts) > 0:
        drawn = steps_of(rng, shape, cuts, -0.22, 0.18) * drawn
    return jnp.clip(drawn, min=-reach, max=reach).astype(held_as)


def setup_inputs(seed: int = 0) -> dict:
    key_list = jax.random.split(jax.random.key(seed), 5)
    return {
        "landmarks": normal_values(key_list[0], (LANDMARKS, DIM), 1.0, 6.0, ((0, 32),), jnp.float32),
        "slab_points": normal_values(key_list[1], (SLAB, DIM), 1.0, 6.0, ((0, 8),), jnp.float32),
        "panel_points": draw_panel_points(jax.random.fold_in(key_list[4], 71), 0),
        "inverse_blocks": draw_inverse_blocks(jax.random.fold_in(key_list[4], 71), 0),
    }


def dot_rows(left_matrix, right_matrix):
    return lax.dot_general(left_matrix.astype(jnp.float32), right_matrix.astype(jnp.float32), (((1,), (1,)), ((), ())), precision=lax.Precision.HIGHEST, preferred_element_type=jnp.float32)

def gaussian(left_points, right_points):
    inner = dot_rows(left_points, right_points)
    left_norms = jnp.sum(left_points * left_points, axis=1)[:, None]
    right_norms = jnp.sum(right_points * right_points, axis=1)[None, :]
    return jnp.exp((2.0 * inner - left_norms - right_norms) / left_points.shape[1])

def factors(points, panel_points, inverse_blocks, first_next):
    first_panel = dot_rows(gaussian(points, panel_points[0]), inverse_blocks[0])
    second_raw = gaussian(points, panel_points[1]) - dot_rows(first_panel, first_next)
    second_panel = dot_rows(second_raw, inverse_blocks[1])
    return jnp.concatenate([first_panel, second_panel], axis=1)

def reference(landmarks, slab_points, panel_points, inverse_blocks):
    first_next = dot_rows(gaussian(panel_points[1], panel_points[0]), inverse_blocks[0])
    slab_factors = factors(slab_points, panel_points, inverse_blocks, first_next)
    blocks = landmarks.reshape(-1, ROWS_DEV, DIM)

    def one_block(landmark_block):
        return gaussian(landmark_block, slab_points) - dot_rows(factors(landmark_block, panel_points, inverse_blocks, first_next), slab_factors)
    result = lax.map(one_block, blocks)
    return result.reshape(-1, slab_points.shape[0])
```

```python
import functools
import math

import jax
import jax.numpy as jnp
from jax import lax
from jax.experimental import pallas as pl
from jax.experimental.pallas import tpu as pltpu
from jax.sharding import PartitionSpec as P

LOG2E = math.log2(math.e)
CHUNK = 160


def dot(left, right, left_dim=1, right_dim=0, precision=None):
    return lax.dot_general(
        left,
        right,
        (((left_dim,), (right_dim,)), ((), ())),
        precision=precision,
        preferred_element_type=jnp.float32,
    )


exact_dot = functools.partial(dot, precision=lax.Precision.HIGHEST)


def split(value):
    high = value.astype(jnp.bfloat16)
    low = (value - high.astype(jnp.float32)).astype(jnp.bfloat16)
    return high, low


def norm_lanes(norm, index, at):
    first = norm.astype(jnp.bfloat16).astype(jnp.float32)
    second = (norm - first).astype(jnp.bfloat16).astype(jnp.float32)
    third = norm - first - second
    lanes = jnp.where(index < 6, 1.0, 0.0)
    lanes = jnp.where(index == at, first, lanes)
    lanes = jnp.where(index == at + 1, second, lanes)
    return jnp.where(index == at + 2, third, lanes).astype(jnp.bfloat16)


def setup_kernel(slab_hbm, panel_hbm, inverse_hbm, points_ref, weights_ref, slab_ref, panel_ref, inverse_ref, sems):
    dim, panel = slab_ref.shape[1], panel_ref.shape[1]
    pairs = ((panel_hbm, panel_ref), (slab_hbm, slab_ref), (inverse_hbm, inverse_ref))
    copies = [pltpu.make_async_copy(source, held, sems.at[i]) for i, (source, held) in enumerate(pairs)]
    for copy in copies:
        copy.start()
    for copy in copies:
        copy.wait()
    panels = [panel_ref[0], panel_ref[1]]
    inverse = [inverse_ref[0], inverse_ref[1]]
    columns = jnp.concatenate([*panels, slab_ref[...]], axis=0).T
    norms = jnp.sum(columns * columns, axis=0, keepdims=True)

    high, low = split(columns * (2.0 * LOG2E / dim))
    index = lax.broadcasted_iota(jnp.int32, columns.shape, 0)
    lanes = norm_lanes(norms * (-LOG2E / dim), index, 3)
    points_ref[...] = jnp.concatenate([high, low, high, lanes], axis=0)

    def gaussian(rows, start):
        row_norms = jnp.sum(rows * rows, axis=1, keepdims=True)
        inner = exact_dot(rows, columns[:, start:])
        return jnp.exp((2.0 * inner - row_norms - norms[:, start:]) / dim)

    firsts = exact_dot(inverse[0], gaussian(panels[0], panel))
    first_next, slab_first = firsts[:, :panel], firsts[:, panel:]
    raw = gaussian(panels[1], 2 * panel) - exact_dot(first_next, slab_first, 0, 0)
    slab_second = exact_dot(inverse[1], raw)
    second = exact_dot(inverse[1], slab_second, 0, 0)
    first = exact_dot(inverse[0], slab_first - exact_dot(first_next, second), 0, 0)
    high, low = split(jnp.concatenate([first, second], axis=0))
    weights_ref[...] = jnp.concatenate([high, low, high], axis=0)


def setup(slab_points, panel_points, inverse_blocks):
    columns, dim = slab_points.shape
    panel = panel_points.shape[1]
    vmem = pl.BlockSpec(memory_space=pltpu.VMEM)
    operands = (slab_points, panel_points, inverse_blocks)
    return pl.pallas_call(
        setup_kernel,
        out_shape=(
            jax.ShapeDtypeStruct((4 * dim, 2 * panel + columns), jnp.bfloat16),
            jax.ShapeDtypeStruct((6 * panel, columns), jnp.bfloat16),
        ),
        in_specs=[pl.BlockSpec(memory_space=pltpu.HBM)] * 3,
        out_specs=(vmem, vmem),
        scratch_shapes=[pltpu.VMEM(x.shape, x.dtype) for x in operands] + [pltpu.SemaphoreType.DMA((3,))],
        compiler_params=pltpu.CompilerParams(vmem_limit_bytes=32 << 20),
        cost_estimate=pl.CostEstimate(
            flops=100 * panel**3, bytes_accessed=4 << 20, transcendentals=3 * panel * panel
        ),
        name="setup",
    )(*operands)


def block_result(points, column_points, weights):
    dim = points.shape[1]
    panels = weights.shape[0] // 3
    high, low = split(points)
    norm = jnp.sum(points * points, axis=1, keepdims=True) * (-LOG2E / dim)
    lanes = norm_lanes(norm, lax.broadcasted_iota(jnp.int32, points.shape, 1), 0)
    kernel = jnp.exp2(dot(jnp.concatenate([high, high, low, lanes], axis=1), column_points))
    high, low = split(kernel[:, :panels])
    return kernel[:, panels:] - dot(jnp.concatenate([high, high, low], axis=1), weights)


def update_kernel(places, block_rows, *refs):
    blocks, (points_ref, weights_ref) = refs[: len(places)], refs[len(places) : len(places) + 2]
    out_ref, held, sems = refs[-3:]
    me = lax.axis_index("col")
    copies, done = [], 0
    for (mask, first_row), block in zip(places, blocks):
        for at in range(0, block.shape[0], CHUNK):
            size = min(CHUNK, block.shape[0] - at)
            held[done : done + size, :] = block_result(
                block[at : at + size, :], points_ref[...], weights_ref[...]
            )
            row = pl.multiple_of(jnp.bitwise_xor(me, mask) * block_rows + first_row + at, 8)
            copy = pltpu.make_async_copy(
                held.at[pl.ds(done, size), :], out_ref.at[pl.ds(row, size), :], sems.at[len(copies)]
            )
            copy.start()
            copies.append(copy)
            done += size
    for copy in copies:
        copy.wait()


def update(out, block_rows, pieces, column_points, weights):
    places = [(mask, first_row) for mask, first_row, _ in pieces]
    blocks = [block for _, _, block in pieces]
    rows = sum(block.shape[0] for block in blocks)
    chunks = sum(-(-block.shape[0] // CHUNK) for block in blocks)
    columns = weights.shape[1]
    vmem = pl.BlockSpec(memory_space=pltpu.VMEM)
    hbm = pl.BlockSpec(memory_space=pltpu.HBM)
    operands = [*blocks, column_points, weights]
    in_specs = [vmem] * (len(blocks) + 2)
    aliases = {}
    if out is not None:
        aliases = {len(operands): 0}
        operands.append(out)
        in_specs.append(hbm)
    return pl.pallas_call(
        functools.partial(update_kernel, places, block_rows),
        out_shape=jax.ShapeDtypeStruct((block_rows * lax.axis_size("col"), columns), jnp.float32),
        in_specs=in_specs,
        out_specs=hbm,
        scratch_shapes=[pltpu.VMEM((rows, columns), jnp.float32), pltpu.SemaphoreType.DMA((chunks,))],
        input_output_aliases=aliases,
        compiler_params=pltpu.CompilerParams(vmem_limit_bytes=32 << 20),
        cost_estimate=pl.CostEstimate(flops=10**10, bytes_accessed=0, transcendentals=0),
        name="update",
    )(*operands)


def swapped(pieces, mask):
    pairs = [(i, i ^ mask) for i in range(lax.axis_size("col"))]
    return [(held ^ mask, row, lax.ppermute(block, "col", pairs)) for held, row, block in pieces]


def cut(pieces, row):
    first = [(mask, at, block[:row]) for mask, at, block in pieces]
    return first, [(mask, at + row, block[row:]) for mask, at, block in pieces]


def after(out, pieces):
    out, *blocks = lax.optimization_barrier((out, *[block for _, _, block in pieces]))
    return out, [(mask, row, block) for (mask, row, _), block in zip(pieces, blocks)]


def local(landmarks, slab_points, panel_points, inverse_blocks):
    size = lax.axis_size("col")
    rows = landmarks.shape[0]
    own = [(0, 0, landmarks)]
    bits = [1 << i for i in reversed(range(1, size.bit_length() - 1))]
    direct = [swapped(own, bit) for bit in bits]
    near = swapped(own, 1)
    column_points, weights = setup(slab_points, panel_points, inverse_blocks)

    def computed(out, pieces):
        return update(out, rows, pieces, column_points, weights)

    out = computed(None, own + near)
    fresh, held = direct[0], []
    for bit, came in zip(bits[1:], direct[1:]):
        out, fresh = after(out, fresh)
        held = held + fresh
        if bit > 2:
            moved = [swapped(held, bit)]
        else:
            moved = [swapped(part, bit) for part in cut(held, rows // 16 * 8)]
        near = swapped(fresh, 1)
        out, came = after(out, came)
        out = computed(out, fresh + near + came + swapped(came, 1))
        held = held + came
        fresh = moved[0]
    out, first = after(out, moved[0])
    near = swapped(first, 1)
    out, second = after(out, moved[1])
    far = swapped(second, 1)
    out = computed(out, first + near + second)
    return computed(out, far)


def solution(mesh):
    in_specs = (P(("row", "col"), None), P("col", None), P(), P())
    out_specs = P("row", "col")
    return jax.shard_map(local, mesh=mesh, in_specs=in_specs, out_specs=out_specs, check_vma=False)
```

```python
import functools
import math

import jax
import jax.numpy as jnp
from jax import lax
from jax.experimental import pallas as pl
from jax.experimental.pallas import tpu as pltpu
from jax.sharding import PartitionSpec as P

LOG2E = math.log2(math.e)
CHUNK = 160
VMEM_BYTES = 16 << 20
SETUP_FLOPS = 17 * 10**8
UPDATE_FLOPS = 10**9
UPDATE_BYTES = 10**7
FENCE_FLOPS = 10**10


def dot(left, right, left_dim=1, right_dim=0, precision=None):
    return lax.dot_general(
        left,
        right,
        (((left_dim,), (right_dim,)), ((), ())),
        precision=precision,
        preferred_element_type=jnp.float32,
    )


exact_dot = functools.partial(dot, precision=lax.Precision.HIGHEST)


def split(value):
    high = value.astype(jnp.bfloat16)
    low = (value - high.astype(jnp.float32)).astype(jnp.bfloat16)
    return high, low


def norm_lanes(norm, index, at):
    first = norm.astype(jnp.bfloat16).astype(jnp.float32)
    second = (norm - first).astype(jnp.bfloat16).astype(jnp.float32)
    third = norm - first - second
    lanes = jnp.where(index < 6, 1.0, 0.0)
    lanes = jnp.where(index == at, first, lanes)
    lanes = jnp.where(index == at + 1, second, lanes)
    return jnp.where(index == at + 2, third, lanes).astype(jnp.bfloat16)


def setup_kernel(slab_hbm, panel_hbm, inverse_hbm, points_ref, weights_ref, out_ref, slab_ref, panel_ref, inverse_ref, sems):
    dim, panel = slab_ref.shape[1], panel_ref.shape[1]
    pairs = ((panel_hbm, panel_ref), (slab_hbm, slab_ref), (inverse_hbm, inverse_ref))
    copies = [pltpu.make_async_copy(source, held, sems.at[i]) for i, (source, held) in enumerate(pairs)]
    for copy in copies:
        copy.start()
    for copy in copies:
        copy.wait()
    panels = [panel_ref[0], panel_ref[1]]
    inverse = [inverse_ref[0], inverse_ref[1]]
    columns = jnp.concatenate([*panels, slab_ref[...]], axis=0).T
    norms = jnp.sum(columns * columns, axis=0, keepdims=True)

    high, low = split(columns * (2.0 * LOG2E / dim))
    index = lax.broadcasted_iota(jnp.int32, columns.shape, 0)
    lanes = norm_lanes(norms * (-LOG2E / dim), index, 3)
    points_ref[...] = jnp.concatenate([high, low, high, lanes], axis=0)

    def gaussian(rows, start):
        row_norms = jnp.sum(rows * rows, axis=1, keepdims=True)
        inner = exact_dot(rows, columns[:, start:])
        return jnp.exp((2.0 * inner - row_norms - norms[:, start:]) / dim)

    firsts = exact_dot(inverse[0], gaussian(panels[0], panel))
    first_next, slab_first = firsts[:, :panel], firsts[:, panel:]
    raw = gaussian(panels[1], 2 * panel) - exact_dot(first_next, slab_first, 0, 0)
    slab_second = exact_dot(inverse[1], raw)
    second = exact_dot(inverse[1], slab_second, 0, 0)
    first = exact_dot(inverse[0], slab_first - exact_dot(first_next, second), 0, 0)
    high, low = split(jnp.concatenate([first, second], axis=0))
    weights_ref[...] = jnp.concatenate([high, low, high], axis=0)


def setup(slab_points, panel_points, inverse_blocks, out_rows):
    columns, dim = slab_points.shape
    panel = panel_points.shape[1]
    vmem = pl.BlockSpec(memory_space=pltpu.VMEM)
    operands = (slab_points, panel_points, inverse_blocks)
    return pl.pallas_call(
        setup_kernel,
        out_shape=(
            jax.ShapeDtypeStruct((4 * dim, 2 * panel + columns), jnp.bfloat16),
            jax.ShapeDtypeStruct((6 * panel, columns), jnp.bfloat16),
            jax.ShapeDtypeStruct((out_rows, columns), jnp.float32),
        ),
        in_specs=[pl.BlockSpec(memory_space=pltpu.HBM)] * 3,
        out_specs=(vmem, vmem, pl.BlockSpec(memory_space=pltpu.HBM)),
        scratch_shapes=[pltpu.VMEM(x.shape, x.dtype) for x in operands] + [pltpu.SemaphoreType.DMA((3,))],
        compiler_params=pltpu.CompilerParams(vmem_limit_bytes=VMEM_BYTES),
        cost_estimate=pl.CostEstimate(
            flops=SETUP_FLOPS, bytes_accessed=4 << 20, transcendentals=3 * panel * panel
        ),
        name="setup",
    )(*operands)


def block_result(points, column_points, weights):
    dim = points.shape[1]
    panels = weights.shape[0] // 3
    high, low = split(points)
    norm = jnp.sum(points * points, axis=1, keepdims=True) * (-LOG2E / dim)
    lanes = norm_lanes(norm, lax.broadcasted_iota(jnp.int32, points.shape, 1), 0)
    kernel = jnp.exp2(dot(jnp.concatenate([high, high, low, lanes], axis=1), column_points))
    high, low = split(kernel[:, :panels])
    return kernel[:, panels:] - dot(jnp.concatenate([high, high, low], axis=1), weights)


def chunks_of(places):
    done, chunks = 0, []
    for mask, first_row, rows in places:
        for at in range(0, rows, CHUNK):
            size = min(CHUNK, rows - at)
            chunks.append((done, mask, first_row + at, size))
            done += size
    return chunks


def update_kernel(places, before, last, block_rows, *refs):
    index_ref, refs = refs[0], refs[1:]
    blocks, (points_ref, weights_ref) = refs[: len(places)], refs[len(places) : len(places) + 2]
    me = index_ref[0]
    out_ref, tile_ref, sems = refs[-3:]
    held_ref = refs[len(places) + 2] if before else None
    copies = []

    def send(source, chunk):
        first, mask, row, size = chunk
        row = pl.multiple_of(jnp.bitwise_xor(me, mask) * block_rows + row, 8)
        copy = pltpu.make_async_copy(
            source.at[pl.ds(first, size), :], out_ref.at[pl.ds(row, size), :], sems.at[len(copies)]
        )
        copy.start()
        copies.append(copy)

    done = 0
    if before:
        for mask, first_row, size in before:
            send(held_ref, (done, mask, first_row, size))
            done += size
    chunks = chunks_of(places)
    piece, used = 0, 0
    for chunk in chunks:
        first, _, _, size = chunk
        if used == places[piece][2]:
            piece, used = piece + 1, 0
        tile_ref[first : first + size, :] = block_result(
            blocks[piece][used : used + size, :], points_ref[...], weights_ref[...]
        )
        used += size
        if last:
            send(tile_ref, chunk)
    for copy in copies:
        copy.wait()


def update(state, index, block_rows, pieces, column_points, weights, last=False):
    out, tile, before = state
    places = [(mask, first_row, block.shape[0]) for mask, first_row, block in pieces]
    rows = sum(place[2] for place in places)
    columns = weights.shape[1]
    vmem = pl.BlockSpec(memory_space=pltpu.VMEM)
    hbm = pl.BlockSpec(memory_space=pltpu.HBM)
    operands = [index] + [block for _, _, block in pieces] + [column_points, weights]
    if before:
        operands.append(tile)
    in_specs = [pl.BlockSpec(memory_space=pltpu.SMEM)] + [vmem] * (len(operands) - 1) + [hbm]
    operands.append(out)
    out_shape = [jax.ShapeDtypeStruct(out.shape, out.dtype)]
    out_specs = [hbm]
    scratch = []
    if last:
        scratch.append(pltpu.VMEM((rows, columns), jnp.float32))
    else:
        out_shape.append(jax.ShapeDtypeStruct((rows, columns), jnp.float32))
        out_specs.append(vmem)
    copies = len(before) + (len(chunks_of(places)) if last else 0)
    scratch.append(pltpu.SemaphoreType.DMA((max(copies, 1),)))
    result = pl.pallas_call(
        functools.partial(update_kernel, places, before, last, block_rows),
        out_shape=out_shape,
        in_specs=in_specs,
        out_specs=out_specs,
        scratch_shapes=scratch,
        input_output_aliases={len(operands) - 1: 0},
        compiler_params=pltpu.CompilerParams(vmem_limit_bytes=VMEM_BYTES),
        cost_estimate=pl.CostEstimate(flops=UPDATE_FLOPS, bytes_accessed=UPDATE_BYTES, transcendentals=0),
        name="update",
    )(*operands)
    if last:
        return result[0]
    return result[0], result[1], places


def fence(out):
    hbm = pl.BlockSpec(memory_space=pltpu.HBM)
    return pl.pallas_call(
        lambda held_ref, out_ref: None,
        out_shape=jax.ShapeDtypeStruct(out.shape, out.dtype),
        in_specs=[hbm],
        out_specs=hbm,
        input_output_aliases={0: 0},
        cost_estimate=pl.CostEstimate(flops=FENCE_FLOPS, bytes_accessed=0, transcendentals=0),
        name="fence",
    )(out)


def swapped(pieces, mask):
    pairs = [(i, i ^ mask) for i in range(lax.axis_size("col"))]
    return [(held ^ mask, row, lax.ppermute(block, "col", pairs)) for held, row, block in pieces]


def cut(pieces, row):
    first = [(mask, at, block[:row]) for mask, at, block in pieces]
    return first, [(mask, at + row, block[row:]) for mask, at, block in pieces]


def after(state, pieces):
    out, *blocks = lax.optimization_barrier((state[0], *[block for _, _, block in pieces]))
    return (out, *state[1:]), [(mask, row, block) for (mask, row, _), block in zip(pieces, blocks)]


def local(landmarks, slab_points, panel_points, inverse_blocks):
    size = lax.axis_size("col")
    rows = landmarks.shape[0]
    index = lax.axis_index("col").astype(jnp.int32).reshape(1)
    own = [(0, 0, landmarks)]
    bits = [1 << i for i in reversed(range(1, size.bit_length() - 1))]
    fresh = [swapped(half, bits[0]) for half in cut(own, rows // 16 * 8)]
    direct = [swapped(own, bit) for bit in bits[1:]]
    pending = own + swapped(own, 1)
    column_points, weights, out = setup(slab_points, panel_points, inverse_blocks, rows * size)
    state = (out, None, [])

    def computed(state, pieces, last=False):
        return update(state, index, rows, pieces, column_points, weights, last)

    moving = [[], []]
    for bit, close in zip(bits[1:], direct):
        state, first = after(state, fresh[0])
        moving[0] = moving[0] + first
        first_on = swapped(moving[0], bit)
        state = (fence(state[0]), *state[1:])
        near = swapped(first, 1)
        state = computed(state, pending)
        state = computed(state, first + near)

        state, second = after(state, fresh[1] + close)
        moving[1] = moving[1] + second[: len(fresh[1])]
        second_on = swapped(moving[1], bit)
        pending = swapped(second, 1)
        moving[1] = moving[1] + second[len(fresh[1]) :]
        state = (fence(state[0]), *state[1:])
        state = computed(state, second)
        fresh = [first_on, second_on]

    state, first = after(state, fresh[0])
    near = swapped(first, 1)
    state = computed(state, pending)
    state, second = after(state, fresh[1])
    far = swapped(second, 1)
    state = computed(state, first + near + second)
    return computed(state, far, last=True)


def solution(mesh):
    in_specs = (P(("row", "col"), None), P("col", None), P(), P())
    out_specs = P("row", "col")
    return jax.shard_map(local, mesh=mesh, in_specs=in_specs, out_specs=out_specs, check_vma=False)
```

```python
import functools
import math

import jax
import jax.numpy as jnp
from jax import lax
from jax.experimental import pallas as pl
from jax.experimental.pallas import tpu as pltpu
from jax.sharding import PartitionSpec as P

LOG2E = math.log2(math.e)
CHUNK = 160
VMEM_BYTES = 16 << 20
SETUP_FLOPS = 17 * 10**8
UPDATE_FLOPS = 10**10
UPDATE_BYTES = 10**7
FENCE_FLOPS = 10**10


def dot(left, right, left_dim=1, right_dim=0, precision=None):
    return lax.dot_general(
        left,
        right,
        (((left_dim,), (right_dim,)), ((), ())),
        precision=precision,
        preferred_element_type=jnp.float32,
    )


exact_dot = functools.partial(dot, precision=lax.Precision.HIGHEST)


def split(value):
    high = value.astype(jnp.bfloat16)
    low = (value - high.astype(jnp.float32)).astype(jnp.bfloat16)
    return high, low


def norm_lanes(norm, index, at):
    first = norm.astype(jnp.bfloat16).astype(jnp.float32)
    second = (norm - first).astype(jnp.bfloat16).astype(jnp.float32)
    third = norm - first - second
    lanes = jnp.where(index < 6, 1.0, 0.0)
    lanes = jnp.where(index == at, first, lanes)
    lanes = jnp.where(index == at + 1, second, lanes)
    return jnp.where(index == at + 2, third, lanes).astype(jnp.bfloat16)


def setup_kernel(slab_hbm, panel_hbm, inverse_hbm, points_ref, weights_ref, out_ref, slab_ref, panel_ref, inverse_ref, sems):
    dim, panel = slab_ref.shape[1], panel_ref.shape[1]
    pairs = ((panel_hbm, panel_ref), (slab_hbm, slab_ref), (inverse_hbm, inverse_ref))
    copies = [pltpu.make_async_copy(source, held, sems.at[i]) for i, (source, held) in enumerate(pairs)]
    for copy in copies:
        copy.start()
    for copy in copies:
        copy.wait()
    panels = [panel_ref[0], panel_ref[1]]
    inverse = [inverse_ref[0], inverse_ref[1]]
    columns = jnp.concatenate([*panels, slab_ref[...]], axis=0).T
    norms = jnp.sum(columns * columns, axis=0, keepdims=True)

    high, low = split(columns * (2.0 * LOG2E / dim))
    index = lax.broadcasted_iota(jnp.int32, columns.shape, 0)
    lanes = norm_lanes(norms * (-LOG2E / dim), index, 3)
    points_ref[...] = jnp.concatenate([high, low, high, lanes], axis=0)

    def gaussian(rows, start):
        row_norms = jnp.sum(rows * rows, axis=1, keepdims=True)
        inner = exact_dot(rows, columns[:, start:])
        return jnp.exp((2.0 * inner - row_norms - norms[:, start:]) / dim)

    firsts = exact_dot(inverse[0], gaussian(panels[0], panel))
    first_next, slab_first = firsts[:, :panel], firsts[:, panel:]
    raw = gaussian(panels[1], 2 * panel) - exact_dot(first_next, slab_first, 0, 0)
    slab_second = exact_dot(inverse[1], raw)
    second = exact_dot(inverse[1], slab_second, 0, 0)
    first = exact_dot(inverse[0], slab_first - exact_dot(first_next, second), 0, 0)
    high, low = split(jnp.concatenate([first, second], axis=0))
    weights_ref[...] = jnp.concatenate([high, low, high], axis=0)


def setup(slab_points, panel_points, inverse_blocks, out_rows):
    columns, dim = slab_points.shape
    panel = panel_points.shape[1]
    vmem = pl.BlockSpec(memory_space=pltpu.VMEM)
    operands = (slab_points, panel_points, inverse_blocks)
    operands = [pltpu.with_memory_space_constraint(x, pltpu.HBM) for x in operands]
    return pl.pallas_call(
        setup_kernel,
        out_shape=(
            jax.ShapeDtypeStruct((4 * dim, 2 * panel + columns), jnp.bfloat16),
            jax.ShapeDtypeStruct((6 * panel, columns), jnp.bfloat16),
            jax.ShapeDtypeStruct((out_rows, columns), jnp.float32),
        ),
        in_specs=[pl.BlockSpec(memory_space=pltpu.HBM)] * 3,
        out_specs=(vmem, vmem, pl.BlockSpec(memory_space=pltpu.HBM)),
        scratch_shapes=[pltpu.VMEM(x.shape, x.dtype) for x in operands] + [pltpu.SemaphoreType.DMA((3,))],
        compiler_params=pltpu.CompilerParams(vmem_limit_bytes=VMEM_BYTES),
        cost_estimate=pl.CostEstimate(
            flops=SETUP_FLOPS, bytes_accessed=4 << 20, transcendentals=3 * panel * panel
        ),
        name="setup",
    )(*operands)


def block_result(points, column_points, weights):
    dim = points.shape[1]
    panels = weights.shape[0] // 3
    high, low = split(points)
    norm = jnp.sum(points * points, axis=1, keepdims=True) * (-LOG2E / dim)
    lanes = norm_lanes(norm, lax.broadcasted_iota(jnp.int32, points.shape, 1), 0)
    kernel = jnp.exp2(dot(jnp.concatenate([high, high, low, lanes], axis=1), column_points))
    high, low = split(kernel[:, :panels])
    return kernel[:, panels:] - dot(jnp.concatenate([high, high, low], axis=1), weights)


def chunks_of(places):
    done, chunks = 0, []
    for mask, first_row, rows in places:
        for at in range(0, rows, CHUNK):
            size = min(CHUNK, rows - at)
            chunks.append((done, mask, first_row + at, size))
            done += size
    return chunks


def update_kernel(places, before, now, block_rows, *refs):
    index_ref, refs = refs[0], refs[1:]
    blocks, (points_ref, weights_ref) = refs[: len(places)], refs[len(places) : len(places) + 2]
    me = index_ref[0]
    out_ref, tile_ref, sems = refs[-3:]
    held_ref = refs[len(places) + 2] if before else None
    copies = []

    def send(source, chunk):
        first, mask, row, size = chunk
        row = pl.multiple_of(jnp.bitwise_xor(me, mask) * block_rows + row, 8)
        copy = pltpu.make_async_copy(
            source.at[pl.ds(first, size), :], out_ref.at[pl.ds(row, size), :], sems.at[len(copies)]
        )
        copy.start()
        copies.append(copy)

    done = 0
    if before:
        for mask, first_row, size in before:
            send(held_ref, (done, mask, first_row, size))
            done += size
    chunks = chunks_of(places)
    piece, used = 0, 0
    for chunk in chunks:
        first, _, _, size = chunk
        if used == places[piece][2]:
            piece, used = piece + 1, 0
        tile_ref[first : first + size, :] = block_result(
            blocks[piece][used : used + size, :], points_ref[...], weights_ref[...]
        )
        used += size
        if now:
            send(tile_ref, chunk)
    for copy in copies:
        copy.wait()


def update(state, index, block_rows, pieces, column_points, weights, now=False):
    out, tile, before = state
    places = [(mask, first_row, block.shape[0]) for mask, first_row, block in pieces]
    rows = sum(place[2] for place in places)
    columns = weights.shape[1]
    vmem = pl.BlockSpec(memory_space=pltpu.VMEM)
    hbm = pl.BlockSpec(memory_space=pltpu.HBM)
    operands = [index] + [block for _, _, block in pieces] + [column_points, weights]
    if before:
        operands.append(tile)
    in_specs = [pl.BlockSpec(memory_space=pltpu.SMEM)] + [vmem] * (len(operands) - 1) + [hbm]
    operands.append(out)
    out_shape = [jax.ShapeDtypeStruct(out.shape, out.dtype)]
    out_specs = [hbm]
    scratch = []
    if now:
        scratch.append(pltpu.VMEM((rows, columns), jnp.float32))
    else:
        out_shape.append(jax.ShapeDtypeStruct((rows, columns), jnp.float32))
        out_specs.append(vmem)
    copies = len(before) + (len(chunks_of(places)) if now else 0)
    scratch.append(pltpu.SemaphoreType.DMA((max(copies, 1),)))
    result = pl.pallas_call(
        functools.partial(update_kernel, places, before, now, block_rows),
        out_shape=out_shape,
        in_specs=in_specs,
        out_specs=out_specs,
        scratch_shapes=scratch,
        input_output_aliases={len(operands) - 1: 0},
        compiler_params=pltpu.CompilerParams(vmem_limit_bytes=VMEM_BYTES),
        cost_estimate=pl.CostEstimate(flops=UPDATE_FLOPS, bytes_accessed=UPDATE_BYTES, transcendentals=0),
        name="update",
    )(*operands)
    if now:
        return result[0], None, []
    return result[0], result[1], places


def parts_kernel(rows_hbm, first_ref, second_ref, sems):
    half = first_ref.shape[0]
    copies = [
        pltpu.make_async_copy(rows_hbm.at[pl.ds(0, half), :], first_ref, sems.at[0]),
        pltpu.make_async_copy(rows_hbm.at[pl.ds(half, second_ref.shape[0]), :], second_ref, sems.at[1]),
    ]
    for copy in copies:
        copy.start()
    for copy in copies:
        copy.wait()


def parts(rows, half):
    vmem = pl.BlockSpec(memory_space=pltpu.VMEM)
    count, dim = rows.shape
    shapes = ((half, dim), (count - half, dim))
    return pl.pallas_call(
        parts_kernel,
        out_shape=tuple(jax.ShapeDtypeStruct(shape, rows.dtype) for shape in shapes),
        in_specs=[pl.BlockSpec(memory_space=pltpu.HBM)],
        out_specs=(vmem, vmem),
        scratch_shapes=[pltpu.SemaphoreType.DMA((2,))],
        compiler_params=pltpu.CompilerParams(vmem_limit_bytes=VMEM_BYTES),
        cost_estimate=pl.CostEstimate(flops=0, bytes_accessed=10**6, transcendentals=0),
        name="parts",
    )(pltpu.with_memory_space_constraint(rows, pltpu.HBM))


def fence(out):
    hbm = pl.BlockSpec(memory_space=pltpu.HBM)
    return pl.pallas_call(
        lambda held_ref, out_ref: None,
        out_shape=jax.ShapeDtypeStruct(out.shape, out.dtype),
        in_specs=[hbm],
        out_specs=hbm,
        input_output_aliases={0: 0},
        cost_estimate=pl.CostEstimate(flops=FENCE_FLOPS, bytes_accessed=0, transcendentals=0),
        name="fence",
    )(out)


def swapped(pieces, mask):
    pairs = [(i, i ^ mask) for i in range(lax.axis_size("col"))]
    return [(held ^ mask, row, lax.ppermute(block, "col", pairs)) for held, row, block in pieces]


def after(state, pieces):
    out, *blocks = lax.optimization_barrier((state[0], *[block for _, _, block in pieces]))
    return (out, *state[1:]), [(mask, row, block) for (mask, row, _), block in zip(pieces, blocks)]


def fenced(state):
    return (fence(state[0]), *state[1:])


def local(landmarks, slab_points, panel_points, inverse_blocks):
    size = lax.axis_size("col")
    rows = landmarks.shape[0]
    half = rows // 16 * 8
    index = lax.axis_index("col").astype(jnp.int32).reshape(1)
    own = [(0, 0, landmarks)]
    upper, lower = parts(landmarks, half)
    halves = [(0, 0, upper)], [(0, half, lower)]
    bits = [1 << i for i in reversed(range(1, size.bit_length() - 1))]
    fresh = [swapped(pieces, bits[0]) for pieces in halves]
    direct = [swapped(own, bit) for bit in bits[1:]]
    near_own = swapped(own, 1)
    column_points, weights, out = setup(slab_points, panel_points, inverse_blocks, rows * size)
    state = (out, None, [])

    def computed(state, pieces, now=False):
        return update(state, index, rows, pieces, column_points, weights, now)

    moving = [[], []]
    pending = halves[0] + halves[1] + near_own
    for bit, close in zip(bits[1:], direct):
        state, first = after(state, fresh[0])
        moving[0] = moving[0] + first
        first_on = swapped(moving[0], bit)
        state = fenced(state)
        near = swapped(first, 1)
        state = computed(state, pending, now=True)
        state = computed(state, first + near, now=True)

        state, second = after(state, fresh[1])
        moving[1] = moving[1] + second
        second_on = swapped(moving[1], bit)
        near = swapped(second, 1)
        state = fenced(state)
        state, close = after(state, close)
        moving[1] = moving[1] + close
        pending = near + swapped(close, 1)
        state = computed(state, second + close)
        fresh = [first_on, second_on]

    state, first = after(state, fresh[0])
    near = swapped(first, 1)
    state = computed(state, pending + first)
    state, second = after(state, fresh[1])
    far = swapped(second, 1)
    state = computed(state, second)
    return computed(state, near + far, now=True)[0]


def solution(mesh):
    in_specs = (P(("row", "col"), None), P("col", None), P(), P())
    out_specs = P("row", "col")
    return jax.shard_map(local, mesh=mesh, in_specs=in_specs, out_specs=out_specs, check_vma=False)
```

```python
import functools
import math

import jax
import jax.numpy as jnp
from jax import lax
from jax.experimental import pallas as pl
from jax.experimental.pallas import tpu as pltpu
from jax.sharding import PartitionSpec as P

LOG2E = math.log2(math.e)
CHUNK = 160
VMEM_BYTES = 16 << 20
SETUP_FLOPS = 17 * 10**8
UPDATE_FLOPS = 10**10
UPDATE_BYTES = 10**7
FENCE_FLOPS = 10**10


def dot(left, right, left_dim=1, right_dim=0, precision=None):
    return lax.dot_general(
        left,
        right,
        (((left_dim,), (right_dim,)), ((), ())),
        precision=precision,
        preferred_element_type=jnp.float32,
    )


exact_dot = functools.partial(dot, precision=lax.Precision.HIGHEST)


def split(value):
    high = value.astype(jnp.bfloat16)
    low = (value - high.astype(jnp.float32)).astype(jnp.bfloat16)
    return high, low


def norm_lanes(norm, index, at):
    first = norm.astype(jnp.bfloat16).astype(jnp.float32)
    second = (norm - first).astype(jnp.bfloat16).astype(jnp.float32)
    third = norm - first - second
    lanes = jnp.where(index < 6, 1.0, 0.0)
    lanes = jnp.where(index == at, first, lanes)
    lanes = jnp.where(index == at + 1, second, lanes)
    return jnp.where(index == at + 2, third, lanes).astype(jnp.bfloat16)


def setup_kernel(slab_hbm, panel_hbm, inverse_hbm, points_ref, weights_ref, out_ref, slab_ref, panel_ref, inverse_ref, sems):
    dim, panel = slab_ref.shape[1], panel_ref.shape[1]
    pairs = ((panel_hbm, panel_ref), (slab_hbm, slab_ref), (inverse_hbm, inverse_ref))
    copies = [pltpu.make_async_copy(source, held, sems.at[i]) for i, (source, held) in enumerate(pairs)]
    for copy in copies:
        copy.start()
    for copy in copies:
        copy.wait()
    panels = [panel_ref[0], panel_ref[1]]
    inverse = [inverse_ref[0], inverse_ref[1]]
    columns = jnp.concatenate([*panels, slab_ref[...]], axis=0).T
    norms = jnp.sum(columns * columns, axis=0, keepdims=True)

    high, low = split(columns * (2.0 * LOG2E / dim))
    index = lax.broadcasted_iota(jnp.int32, columns.shape, 0)
    lanes = norm_lanes(norms * (-LOG2E / dim), index, 3)
    points_ref[...] = jnp.concatenate([high, low, high, lanes], axis=0)

    def gaussian(rows, start):
        row_norms = jnp.sum(rows * rows, axis=1, keepdims=True)
        inner = exact_dot(rows, columns[:, start:])
        return jnp.exp((2.0 * inner - row_norms - norms[:, start:]) / dim)

    firsts = exact_dot(inverse[0], gaussian(panels[0], panel))
    first_next, slab_first = firsts[:, :panel], firsts[:, panel:]
    raw = gaussian(panels[1], 2 * panel) - exact_dot(first_next, slab_first, 0, 0)
    slab_second = exact_dot(inverse[1], raw)
    second = exact_dot(inverse[1], slab_second, 0, 0)
    first = exact_dot(inverse[0], slab_first - exact_dot(first_next, second), 0, 0)
    high, low = split(jnp.concatenate([first, second], axis=0))
    weights_ref[...] = jnp.concatenate([high, low, high], axis=0)


def setup(slab_points, panel_points, inverse_blocks, out_rows):
    columns, dim = slab_points.shape
    panel = panel_points.shape[1]
    vmem = pl.BlockSpec(memory_space=pltpu.VMEM)
    operands = (slab_points, panel_points, inverse_blocks)
    operands = [pltpu.with_memory_space_constraint(x, pltpu.HBM) for x in operands]
    return pl.pallas_call(
        setup_kernel,
        out_shape=(
            jax.ShapeDtypeStruct((4 * dim, 2 * panel + columns), jnp.bfloat16),
            jax.ShapeDtypeStruct((6 * panel, columns), jnp.bfloat16),
            jax.ShapeDtypeStruct((out_rows, columns), jnp.float32),
        ),
        in_specs=[pl.BlockSpec(memory_space=pltpu.HBM)] * 3,
        out_specs=(vmem, vmem, pl.BlockSpec(memory_space=pltpu.HBM)),
        scratch_shapes=[pltpu.VMEM(x.shape, x.dtype) for x in operands] + [pltpu.SemaphoreType.DMA((3,))],
        compiler_params=pltpu.CompilerParams(vmem_limit_bytes=VMEM_BYTES),
        cost_estimate=pl.CostEstimate(
            flops=SETUP_FLOPS, bytes_accessed=4 << 20, transcendentals=3 * panel * panel
        ),
        name="setup",
    )(*operands)


def block_result(points, column_points, weights):
    dim = points.shape[1]
    panels = weights.shape[0] // 3
    high, low = split(points)
    norm = jnp.sum(points * points, axis=1, keepdims=True) * (-LOG2E / dim)
    lanes = norm_lanes(norm, lax.broadcasted_iota(jnp.int32, points.shape, 1), 0)
    kernel = jnp.exp2(dot(jnp.concatenate([high, high, low, lanes], axis=1), column_points))
    high, low = split(kernel[:, :panels])
    return kernel[:, panels:] - dot(jnp.concatenate([high, high, low], axis=1), weights)


def chunks_of(places):
    done, chunks = 0, []
    for mask, first_row, rows in places:
        for at in range(0, rows, CHUNK):
            size = min(CHUNK, rows - at)
            chunks.append((done, mask, first_row + at, size))
            done += size
    return chunks


def update_kernel(places, before, now, block_rows, *refs):
    index_ref, refs = refs[0], refs[1:]
    blocks, (points_ref, weights_ref) = refs[: len(places)], refs[len(places) : len(places) + 2]
    me = index_ref[0]
    out_ref, tile_ref, sems = refs[-3:]
    held_ref = refs[len(places) + 2] if before else None
    copies = []

    def send(source, chunk):
        first, mask, row, size = chunk
        row = pl.multiple_of(jnp.bitwise_xor(me, mask) * block_rows + row, 8)
        copy = pltpu.make_async_copy(
            source.at[pl.ds(first, size), :], out_ref.at[pl.ds(row, size), :], sems.at[len(copies)]
        )
        copy.start()
        copies.append(copy)

    done = 0
    if before:
        for mask, first_row, size in before:
            send(held_ref, (done, mask, first_row, size))
            done += size
    chunks = chunks_of(places)
    piece, used = 0, 0
    for chunk in chunks:
        first, _, _, size = chunk
        if used == places[piece][2]:
            piece, used = piece + 1, 0
        tile_ref[first : first + size, :] = block_result(
            blocks[piece][used : used + size, :], points_ref[...], weights_ref[...]
        )
        used += size
        mask, first_row, rows = places[piece]
        if now and piece == len(places) - 1:
            send(tile_ref, chunk)
        elif now and used == rows:
            send(tile_ref, (first + size - rows, mask, first_row, rows))
    for copy in copies:
        copy.wait()


def update(state, index, block_rows, pieces, column_points, weights, now=False):
    out, tile, before = state
    places = [(mask, first_row, block.shape[0]) for mask, first_row, block in pieces]
    rows = sum(place[2] for place in places)
    columns = weights.shape[1]
    vmem = pl.BlockSpec(memory_space=pltpu.VMEM)
    hbm = pl.BlockSpec(memory_space=pltpu.HBM)
    operands = [index] + [block for _, _, block in pieces] + [column_points, weights]
    if before:
        operands.append(tile)
    in_specs = [pl.BlockSpec(memory_space=pltpu.SMEM)] + [vmem] * (len(operands) - 1) + [hbm]
    operands.append(out)
    out_shape = [jax.ShapeDtypeStruct(out.shape, out.dtype)]
    out_specs = [hbm]
    scratch = []
    if now:
        scratch.append(pltpu.VMEM((rows, columns), jnp.float32))
    else:
        out_shape.append(jax.ShapeDtypeStruct((rows, columns), jnp.float32))
        out_specs.append(vmem)
    copies = len(before) + (len(chunks_of(places)) if now else 0)
    scratch.append(pltpu.SemaphoreType.DMA((max(copies, 1),)))
    result = pl.pallas_call(
        functools.partial(update_kernel, places, before, now, block_rows),
        out_shape=out_shape,
        in_specs=in_specs,
        out_specs=out_specs,
        scratch_shapes=scratch,
        input_output_aliases={len(operands) - 1: 0},
        compiler_params=pltpu.CompilerParams(vmem_limit_bytes=VMEM_BYTES),
        cost_estimate=pl.CostEstimate(flops=UPDATE_FLOPS, bytes_accessed=UPDATE_BYTES, transcendentals=0),
        name="update",
    )(*operands)
    if now:
        return result[0], None, []
    return result[0], result[1], places


def parts_kernel(rows_hbm, first_ref, second_ref, sems):
    half = first_ref.shape[0]
    copies = [
        pltpu.make_async_copy(rows_hbm.at[pl.ds(0, half), :], first_ref, sems.at[0]),
        pltpu.make_async_copy(rows_hbm.at[pl.ds(half, second_ref.shape[0]), :], second_ref, sems.at[1]),
    ]
    for copy in copies:
        copy.start()
    for copy in copies:
        copy.wait()


def parts(rows, half):
    vmem = pl.BlockSpec(memory_space=pltpu.VMEM)
    count, dim = rows.shape
    shapes = ((half, dim), (count - half, dim))
    return pl.pallas_call(
        parts_kernel,
        out_shape=tuple(jax.ShapeDtypeStruct(shape, rows.dtype) for shape in shapes),
        in_specs=[pl.BlockSpec(memory_space=pltpu.HBM)],
        out_specs=(vmem, vmem),
        scratch_shapes=[pltpu.SemaphoreType.DMA((2,))],
        compiler_params=pltpu.CompilerParams(vmem_limit_bytes=VMEM_BYTES),
        cost_estimate=pl.CostEstimate(flops=0, bytes_accessed=10**6, transcendentals=0),
        name="parts",
    )(pltpu.with_memory_space_constraint(rows, pltpu.HBM))


def fence(out):
    hbm = pl.BlockSpec(memory_space=pltpu.HBM)
    return pl.pallas_call(
        lambda held_ref, out_ref: None,
        out_shape=jax.ShapeDtypeStruct(out.shape, out.dtype),
        in_specs=[hbm],
        out_specs=hbm,
        input_output_aliases={0: 0},
        cost_estimate=pl.CostEstimate(flops=FENCE_FLOPS, bytes_accessed=0, transcendentals=0),
        name="fence",
    )(out)


def swapped(pieces, mask):
    pairs = [(i, i ^ mask) for i in range(lax.axis_size("col"))]
    return [(held ^ mask, row, lax.ppermute(block, "col", pairs)) for held, row, block in pieces]


def after(state, pieces):
    out, *blocks = lax.optimization_barrier((state[0], *[block for _, _, block in pieces]))
    return (out, *state[1:]), [(mask, row, block) for (mask, row, _), block in zip(pieces, blocks)]


def fenced(state):
    return (fence(state[0]), *state[1:])


def local(landmarks, slab_points, panel_points, inverse_blocks):
    size = lax.axis_size("col")
    rows = landmarks.shape[0]
    half = rows // 16 * 8
    index = lax.axis_index("col").astype(jnp.int32).reshape(1)
    own = [(0, 0, landmarks)]
    upper, lower = parts(landmarks, half)
    halves = [(0, 0, upper)], [(0, half, lower)]
    bits = [1 << i for i in reversed(range(1, size.bit_length() - 1))]
    fresh = [swapped(pieces, bits[0]) for pieces in halves]
    direct = [swapped(own, bit) for bit in bits[1:]]
    near_own = swapped(own, 1)
    column_points, weights, out = setup(slab_points, panel_points, inverse_blocks, rows * size)
    state = (out, None, [])

    def computed(state, pieces, now=False):
        return update(state, index, rows, pieces, column_points, weights, now)

    moving = [[], []]
    pending = halves[0] + halves[1] + near_own
    for bit, close in zip(bits[1:], direct):
        state = computed(state, pending, now=True)
        state, first = after(state, fresh[0])
        moving[0] = moving[0] + first
        first_on = swapped(moving[0], bit)
        near = swapped(first, 1)
        state = fenced(state)
        state = computed(state, first + near, now=True)

        state, second = after(state, fresh[1])
        moving[1] = moving[1] + second
        second_on = swapped(moving[1], bit)
        near = swapped(second, 1)
        state = fenced(state)
        state, close = after(state, close)
        moving[1] = moving[1] + close
        pending = near + swapped(close, 1)
        state = computed(state, second + close)
        fresh = [first_on, second_on]

    state, first = after(state, fresh[0])
    near = swapped(first, 1)
    state = computed(state, pending + first)
    state, second = after(state, fresh[1])
    far = swapped(second, 1)
    state = computed(state, second)
    return computed(state, near + far, now=True)[0]


def solution(mesh):
    in_specs = (P(("row", "col"), None), P("col", None), P(), P())
    out_specs = P("row", "col")
    return jax.shard_map(local, mesh=mesh, in_specs=in_specs, out_specs=out_specs, check_vma=False)
```

```python
import functools
import math

import jax
import jax.numpy as jnp
from jax import lax
from jax.experimental import pallas as pl
from jax.experimental.pallas import tpu as pltpu
from jax.sharding import PartitionSpec as P

LOG2E = math.log2(math.e)
CHUNK = 160
VMEM_BYTES = 16 << 20
SETUP_FLOPS = 17 * 10**8
UPDATE_FLOPS = 10**10
UPDATE_BYTES = 10**7
FENCE_FLOPS = 10**10


def dot(left, right, left_dim=1, right_dim=0, precision=None):
    return lax.dot_general(
        left,
        right,
        (((left_dim,), (right_dim,)), ((), ())),
        precision=precision,
        preferred_element_type=jnp.float32,
    )


exact_dot = functools.partial(dot, precision=lax.Precision.HIGHEST)


def split(value):
    high = value.astype(jnp.bfloat16)
    low = (value - high.astype(jnp.float32)).astype(jnp.bfloat16)
    return high, low


def norm_lanes(norm, index, at):
    first = norm.astype(jnp.bfloat16).astype(jnp.float32)
    second = (norm - first).astype(jnp.bfloat16).astype(jnp.float32)
    third = norm - first - second
    lanes = jnp.where(index < 6, 1.0, 0.0)
    lanes = jnp.where(index == at, first, lanes)
    lanes = jnp.where(index == at + 1, second, lanes)
    return jnp.where(index == at + 2, third, lanes).astype(jnp.bfloat16)


def setup_kernel(slab_hbm, panel_hbm, inverse_hbm, points_ref, weights_ref, out_ref, slab_ref, panel_ref, inverse_ref, sems):
    dim, panel = slab_ref.shape[1], panel_ref.shape[1]
    pairs = ((panel_hbm, panel_ref), (slab_hbm, slab_ref), (inverse_hbm, inverse_ref))
    copies = [pltpu.make_async_copy(source, held, sems.at[i]) for i, (source, held) in enumerate(pairs)]
    for copy in copies:
        copy.start()
    for copy in copies:
        copy.wait()
    panels = [panel_ref[0], panel_ref[1]]
    inverse = [inverse_ref[0], inverse_ref[1]]
    columns = jnp.concatenate([*panels, slab_ref[...]], axis=0).T
    norms = jnp.sum(columns * columns, axis=0, keepdims=True)

    high, low = split(columns * (2.0 * LOG2E / dim))
    index = lax.broadcasted_iota(jnp.int32, columns.shape, 0)
    lanes = norm_lanes(norms * (-LOG2E / dim), index, 3)
    points_ref[...] = jnp.concatenate([high, low, high, lanes], axis=0)

    def gaussian(rows, start):
        row_norms = jnp.sum(rows * rows, axis=1, keepdims=True)
        inner = exact_dot(rows, columns[:, start:])
        return jnp.exp((2.0 * inner - row_norms - norms[:, start:]) / dim)

    firsts = exact_dot(inverse[0], gaussian(panels[0], panel))
    first_next, slab_first = firsts[:, :panel], firsts[:, panel:]
    raw = gaussian(panels[1], 2 * panel) - exact_dot(first_next, slab_first, 0, 0)
    slab_second = exact_dot(inverse[1], raw)
    second = exact_dot(inverse[1], slab_second, 0, 0)
    first = exact_dot(inverse[0], slab_first - exact_dot(first_next, second), 0, 0)
    high, low = split(jnp.concatenate([first, second], axis=0))
    weights_ref[...] = jnp.concatenate([high, low, high], axis=0)


def setup(slab_points, panel_points, inverse_blocks, out_rows):
    columns, dim = slab_points.shape
    panel = panel_points.shape[1]
    vmem = pl.BlockSpec(memory_space=pltpu.VMEM)
    operands = (slab_points, panel_points, inverse_blocks)
    operands = [pltpu.with_memory_space_constraint(x, pltpu.HBM) for x in operands]
    return pl.pallas_call(
        setup_kernel,
        out_shape=(
            jax.ShapeDtypeStruct((4 * dim, 2 * panel + columns), jnp.bfloat16),
            jax.ShapeDtypeStruct((6 * panel, columns), jnp.bfloat16),
            jax.ShapeDtypeStruct((out_rows, columns), jnp.float32),
        ),
        in_specs=[pl.BlockSpec(memory_space=pltpu.HBM)] * 3,
        out_specs=(vmem, vmem, pl.BlockSpec(memory_space=pltpu.HBM)),
        scratch_shapes=[pltpu.VMEM(x.shape, x.dtype) for x in operands] + [pltpu.SemaphoreType.DMA((3,))],
        compiler_params=pltpu.CompilerParams(vmem_limit_bytes=VMEM_BYTES),
        cost_estimate=pl.CostEstimate(
            flops=SETUP_FLOPS, bytes_accessed=4 << 20, transcendentals=3 * panel * panel
        ),
        name="setup",
    )(*operands)


def block_result(points, column_points, weights):
    dim = points.shape[1]
    panels = weights.shape[0] // 3
    high, low = split(points)
    norm = jnp.sum(points * points, axis=1, keepdims=True) * (-LOG2E / dim)
    lanes = norm_lanes(norm, lax.broadcasted_iota(jnp.int32, points.shape, 1), 0)
    kernel = jnp.exp2(dot(jnp.concatenate([high, high, low, lanes], axis=1), column_points))
    high, low = split(kernel[:, :panels])
    return kernel[:, panels:] - dot(jnp.concatenate([high, high, low], axis=1), weights)


def chunks_of(places):
    done, chunks = 0, []
    for mask, first_row, rows in places:
        for at in range(0, rows, CHUNK):
            size = min(CHUNK, rows - at)
            chunks.append((done, mask, first_row + at, size))
            done += size
    return chunks


def update_kernel(places, before, now, block_rows, *refs):
    index_ref, refs = refs[0], refs[1:]
    blocks, (points_ref, weights_ref) = refs[: len(places)], refs[len(places) : len(places) + 2]
    me = index_ref[0]
    out_ref, tile_ref, sems = refs[-3:]
    held_ref = refs[len(places) + 2] if before else None
    copies = []

    def send(source, chunk):
        first, mask, row, size = chunk
        row = pl.multiple_of(jnp.bitwise_xor(me, mask) * block_rows + row, 8)
        copy = pltpu.make_async_copy(
            source.at[pl.ds(first, size), :], out_ref.at[pl.ds(row, size), :], sems.at[len(copies)]
        )
        copy.start()
        copies.append(copy)

    done = 0
    if before:
        for mask, first_row, size in before:
            send(held_ref, (done, mask, first_row, size))
            done += size
    chunks = chunks_of(places)
    piece, used = 0, 0
    for chunk in chunks:
        first, _, _, size = chunk
        if used == places[piece][2]:
            piece, used = piece + 1, 0
        tile_ref[first : first + size, :] = block_result(
            blocks[piece][used : used + size, :], points_ref[...], weights_ref[...]
        )
        used += size
        mask, first_row, rows = places[piece]
        if now and piece == len(places) - 1:
            send(tile_ref, chunk)
        elif now and used == rows:
            send(tile_ref, (first + size - rows, mask, first_row, rows))
    for copy in copies:
        copy.wait()


def update(state, index, block_rows, pieces, column_points, weights, now=False):
    out, tile, before = state
    places = [(mask, first_row, block.shape[0]) for mask, first_row, block in pieces]
    rows = sum(place[2] for place in places)
    columns = weights.shape[1]
    vmem = pl.BlockSpec(memory_space=pltpu.VMEM)
    hbm = pl.BlockSpec(memory_space=pltpu.HBM)
    operands = [index] + [block for _, _, block in pieces] + [column_points, weights]
    if before:
        operands.append(tile)
    in_specs = [pl.BlockSpec(memory_space=pltpu.SMEM)] + [vmem] * (len(operands) - 1) + [hbm]
    operands.append(out)
    out_shape = [jax.ShapeDtypeStruct(out.shape, out.dtype)]
    out_specs = [hbm]
    scratch = []
    if now:
        scratch.append(pltpu.VMEM((rows, columns), jnp.float32))
    else:
        out_shape.append(jax.ShapeDtypeStruct((rows, columns), jnp.float32))
        out_specs.append(vmem)
    copies = len(before) + (len(chunks_of(places)) if now else 0)
    scratch.append(pltpu.SemaphoreType.DMA((max(copies, 1),)))
    result = pl.pallas_call(
        functools.partial(update_kernel, places, before, now, block_rows),
        out_shape=out_shape,
        in_specs=in_specs,
        out_specs=out_specs,
        scratch_shapes=scratch,
        input_output_aliases={len(operands) - 1: 0},
        compiler_params=pltpu.CompilerParams(vmem_limit_bytes=VMEM_BYTES),
        cost_estimate=pl.CostEstimate(flops=UPDATE_FLOPS, bytes_accessed=UPDATE_BYTES, transcendentals=0),
        name="update",
    )(*operands)
    if now:
        return result[0], None, []
    return result[0], result[1], places


def parts_kernel(rows_hbm, first_ref, second_ref, sems):
    half = first_ref.shape[0]
    copies = [
        pltpu.make_async_copy(rows_hbm.at[pl.ds(0, half), :], first_ref, sems.at[0]),
        pltpu.make_async_copy(rows_hbm.at[pl.ds(half, second_ref.shape[0]), :], second_ref, sems.at[1]),
    ]
    for copy in copies:
        copy.start()
    for copy in copies:
        copy.wait()


def parts(rows, half):
    vmem = pl.BlockSpec(memory_space=pltpu.VMEM)
    count, dim = rows.shape
    shapes = ((half, dim), (count - half, dim))
    return pl.pallas_call(
        parts_kernel,
        out_shape=tuple(jax.ShapeDtypeStruct(shape, rows.dtype) for shape in shapes),
        in_specs=[pl.BlockSpec(memory_space=pltpu.HBM)],
        out_specs=(vmem, vmem),
        scratch_shapes=[pltpu.SemaphoreType.DMA((2,))],
        compiler_params=pltpu.CompilerParams(vmem_limit_bytes=VMEM_BYTES),
        cost_estimate=pl.CostEstimate(flops=0, bytes_accessed=10**6, transcendentals=0),
        name="parts",
    )(pltpu.with_memory_space_constraint(rows, pltpu.HBM))


def fence(out):
    hbm = pl.BlockSpec(memory_space=pltpu.HBM)
    return pl.pallas_call(
        lambda held_ref, out_ref: None,
        out_shape=jax.ShapeDtypeStruct(out.shape, out.dtype),
        in_specs=[hbm],
        out_specs=hbm,
        input_output_aliases={0: 0},
        cost_estimate=pl.CostEstimate(flops=FENCE_FLOPS, bytes_accessed=0, transcendentals=0),
        name="fence",
    )(out)


def swapped(pieces, mask):
    pairs = [(i, i ^ mask) for i in range(lax.axis_size("col"))]
    return [(held ^ mask, row, lax.ppermute(block, "col", pairs)) for held, row, block in pieces]


def after(state, pieces):
    out, *blocks = lax.optimization_barrier((state[0], *[block for _, _, block in pieces]))
    return (out, *state[1:]), [(mask, row, block) for (mask, row, _), block in zip(pieces, blocks)]


def fenced(state):
    return (fence(state[0]), *state[1:])


def local(landmarks, slab_points, panel_points, inverse_blocks):
    size = lax.axis_size("col")
    rows = landmarks.shape[0]
    half = rows // 16 * 8
    index = lax.axis_index("col").astype(jnp.int32).reshape(1)
    own = [(0, 0, landmarks)]
    upper, lower = parts(landmarks, half)
    halves = [(0, 0, upper)], [(0, half, lower)]
    bits = [1 << i for i in reversed(range(1, size.bit_length() - 1))]
    fresh = [swapped(pieces, bits[0]) for pieces in halves]
    direct = [swapped(own, bit) for bit in bits[1:]]
    near_own = swapped(own, 1)
    column_points, weights, out = setup(slab_points, panel_points, inverse_blocks, rows * size)
    state = (out, None, [])

    def computed(state, pieces, now=False):
        return update(state, index, rows, pieces, column_points, weights, now)

    moving = [[], []]
    pending = halves[0] + halves[1] + near_own
    for bit, close in zip(bits[1:], direct):
        state, first = after(state, fresh[0])
        moving[0] = moving[0] + first
        first_on = swapped(moving[0], bit)
        state = fenced(state)
        near = swapped(first, 1)
        state = computed(state, pending, now=True)
        state = computed(state, first + near, now=True)

        state, second = after(state, fresh[1])
        moving[1] = moving[1] + second
        second_on = swapped(moving[1], bit)
        near = swapped(second, 1)
        state = fenced(state)
        state, close = after(state, close)
        moving[1] = moving[1] + close
        pending = near + swapped(close, 1)
        state = computed(state, second + close)
        fresh = [first_on, second_on]

    state, first = after(state, fresh[0])
    near = swapped(first, 1)
    state = computed(state, pending + first)
    state, second = after(state, fresh[1])
    far = swapped(second, 1)
    state = computed(state, second)
    return computed(state, near + far, now=True)[0]


def solution(mesh):
    in_specs = (P(("row", "col"), None), P("col", None), P(), P())
    out_specs = P("row", "col")
    return jax.shard_map(local, mesh=mesh, in_specs=in_specs, out_specs=out_specs, check_vma=False)
```
